32 devices in a mesh: fsdp: 16 (over z, x, core), tp: 2 (over y).
Axes of the slice: x: 2, y: 2, z: 4, core: 2. Of those that a mesh axis runs over, the one named last changes fastest.
Arguments:
- inputs: bfloat16 [16384, 1152], P(('fsdp', 'tp')), may hold values from -6 to 6
- conditions: bfloat16 [16, 1152], P('fsdp'), may hold values from -6 to 6
- modulation_weight: bfloat16 [1152, 6, 1152], P('fsdp', None, 'tp'), may hold values from -0.1875 to 0.1875
- modulation_bias: bfloat16 [6, 1152], P(None, 'tp'), may hold values from -3 to 3
- attention_weight: bfloat16 [1152, 3, 1152], P('fsdp', None, 'tp'), may hold values from -0.1875 to 0.1875
- attention_bias: bfloat16 [2, 1152], P(None, 'tp'), may hold values from -3 to 3
- output_weight: bfloat16 [1152, 1152], P('tp', 'fsdp'), may hold values from -1.5 to 1.5
- output_bias: bfloat16 [1152], replicated, may hold values from -1.75 to 1.75
- up_weight: bfloat16 [1152, 4608], P('fsdp', 'tp'), may hold values from -0.1875 to 0.1875
- up_bias: bfloat16 [4608], P('tp'), may hold values from -3 to 3
- down_weight: bfloat16 [4608, 1152], P('tp', 'fsdp'), may hold values from -0.09375 to 0.09375
- down_bias: bfloat16 [1152], replicated, may hold values from -1.75 to 1.75
- cotangent: bfloat16 [16384, 1152], P(('fsdp', 'tp')), may hold values from -6 to 6
Outputs:
- outputs: bfloat16 [16384, 1152], P(('fsdp', 'tp'))
- grad_inputs: float32 [16384, 1152], P(('fsdp', 'tp'))
- grad_conditions: float32 [16, 1152], P('fsdp')
- grad_modulation_weight: float32 [1152, 6, 1152], P('fsdp', None, 'tp')
- grad_modulation_bias: float32 [6, 1152], P(None, 'tp')
- grad_attention_weight: float32 [1152, 3, 1152], P('fsdp', None, 'tp')
- grad_attention_bias: float32 [2, 1152], P(None, 'tp')
- grad_output_weight: float32 [1152, 1152], P('tp', 'fsdp')
- grad_output_bias: float32 [1152], replicated
- grad_up_weight: float32 [1152, 4608], P('fsdp', 'tp')
- grad_up_bias: float32 [4608], P('tp')
- grad_down_weight: float32 [4608, 1152], P('tp', 'fsdp')
- grad_down_bias: float32 [1152], replicated
The draws below stay inside these ranges and needn't reach their ends.
All inputs are finite; a program needn't handle non-finite values.
Results may differ from the reference program's by a relative error of at most 0.02.
The reference program's roundings to bfloat16 on the way count: a program that leaves them out, or rounds other values in their place, can miss the bound.
Values may be sent and summed in bfloat16 or wider, within the bound.
No kernel may reach another device: no remote copies, remote signals or barrier semaphores. Data moves between devices by JAX's collectives and lax.ppermute only.
A program may use at most 192 MiB of HBM per device.

```python
import jax
import jax.numpy as jnp
from jax import lax

D = 1152
H = 16
HD = 72
FF = 4608
SEQ = 1024
LATENTS = 16
TOKENS = 16384


def steps_of(stream_key, extent, cuts, least, high):
    def one(dim, blocks):
        steps = jax.random.uniform(jax.random.fold_in(jax.random.fold_in(stream_key, 6), dim), (blocks,), jnp.float32, least / len(cuts), high / len(cuts))
        return jnp.repeat(jnp.exp(steps), extent[dim] // blocks).reshape((-1,) + (1,) * (len(extent) - dim - 1))

    loudness = one(*cuts[0])
    for cut in cuts[1:]:
        loudness = loudness * one(*cut)
    return loudness


def gaussian(key, dims, scale, reach, cuts=(), held_as=jnp.bfloat16):
    array = scale * jax.random.normal(key, dims, jnp.float32)
    if cuts:
        array = array * steps_of(key, dims, cuts, -0.22, 0.18)
    return jnp.clip(array, -reach, reach).astype(held_as)


def setup_inputs(seed: int = 0) -> dict:
    splits = jax.random.split(jax.random.key(seed), 14)
    return {
        "inputs": gaussian(splits[0], (TOKENS, D), 1.0, 6.0, ((0, 32),)),
        "conditions": gaussian(splits[1], (LATENTS, D), 1.0, 6.0, ((0, 16),)),
        "modulation_weight": gaussian(splits[2], (D, 6, D), D ** -0.5, 0.1875, ((0, 16), (2, 2))),
        "modulation_bias": gaussian(splits[3], (6, D), 0.5, 3.0, ((1, 2),)),
        "attention_weight": gaussian(splits[4], (D, 3, D), D ** -0.5, 0.1875, ((0, 16), (2, 2))),
        "attention_bias": gaussian(splits[5], (2, D), 0.5, 3.0, ((1, 2),)),
        "output_weight": gaussian(splits[6], (D, D), (D // 64) ** -0.5, 1.5, ((0, 2), (1, 16))),
        "output_bias": gaussian(splits[7], (D,), 0.3, 1.75),
        "up_weight": gaussian(splits[8], (D, FF), D ** -0.5, 0.1875, ((0, 16), (1, 2))),
        "up_bias": gaussian(splits[9], (FF,), 0.5, 3.0, ((0, 2),)),
        "down_weight": gaussian(splits[10], (FF, D), FF ** -0.5, 0.09375, ((0, 2), (1, 16))),
        "down_bias": gaussian(splits[11], (D,), 0.3, 1.75),
        "cotangent": gaussian(splits[12], (TOKENS, D), 1.0, 6.0, ((0, 32),)),
    }


@jax.custom_vjp
def low(v):
    return lax.optimization_barrier(v.astype(jnp.bfloat16)).astype(jnp.float32)

@jax.custom_vjp
def low_back(v):
    return v

def low_keep(v):
    return (low(v), None)

def low_pass(kept, grad):
    return (grad,)

def back_keep(v):
    return (v, None)

def back_low(kept, grad):
    return (low(grad),)
low.defvjp(low_keep, low_pass)
low_back.defvjp(back_keep, back_low)
EPS = 1e-06
HIGH = lax.Precision.HIGHEST

def normalize(values):
    centred = values - lax.optimization_barrier(jnp.mean(values, axis=-1, keepdims=True))
    return centred * lax.rsqrt(lax.optimization_barrier(jnp.mean(centred * centred, axis=-1, keepdims=True)) + EPS)

def attend_latent(packed):
    queries = packed[:, 0].reshape(SEQ, H, HD)
    key_rows = packed[:, 1].reshape(SEQ, H, HD)
    value_rows = packed[:, 2].reshape(SEQ, H, HD)
    scores = low_back(jnp.einsum('qhe,khe->hqk', queries, key_rows, precision=HIGH) * HD ** (-0.5))
    shares = low(jax.nn.softmax(scores, axis=-1))
    return jnp.einsum('hqk,khe->qhe', shares, value_rows, precision=HIGH).reshape(SEQ, D)

def block_latent(params, rows, mod_one):
    attention_weight, attention_bias, output_weight, output_bias, up_weight, up_bias, down_weight, down_bias = params
    first = low(normalize(rows) * (1.0 + mod_one[1]) + mod_one[0])
    packed_bias = jnp.stack([attention_bias[0], jnp.zeros_like(attention_bias[0]), attention_bias[1]])
    packed = low_back(low(jnp.einsum('sd,dkc->skc', first, attention_weight, precision=HIGH) + packed_bias))
    heads_out = low_back(low(attend_latent(packed)))
    attention = low_back(jnp.dot(heads_out, output_weight, precision=HIGH) + output_bias)
    mid = rows + mod_one[2] * attention
    second = low(normalize(mid) * (1.0 + mod_one[4]) + mod_one[3])
    pre = low_back(jnp.dot(second, up_weight, precision=HIGH) + up_bias)
    act = low(jax.nn.gelu(pre, approximate=True))
    feed = low_back(jnp.dot(act, down_weight, precision=HIGH) + down_bias)
    return mid + mod_one[5] * feed

def forward(inputs, conditions, modulation_weight, modulation_bias, attention_weight, attention_bias, output_weight, output_bias, up_weight, up_bias, down_weight, down_bias):
    silu_low = low(jax.nn.silu(conditions))
    modulation = low_back(jnp.einsum('ld,dkc->lkc', silu_low, modulation_weight, precision=HIGH) + modulation_bias)
    rows = inputs.reshape(-1, SEQ, D)
    params = (attention_weight, attention_bias, output_weight, output_bias, up_weight, up_bias, down_weight, down_bias)

    def one_latent(items):
        return block_latent(params, items[0], items[1])
    results = lax.map(jax.checkpoint(one_latent), (rows, modulation))
    return results.reshape(-1, D)

def reference(inputs, conditions, modulation_weight, modulation_bias, attention_weight, attention_bias, output_weight, output_bias, up_weight, up_bias, down_weight, down_bias, cotangent):
    f32 = jnp.float32
    outputs, backward = jax.vjp(forward, inputs.astype(f32), conditions.astype(f32), modulation_weight.astype(f32), modulation_bias.astype(f32), attention_weight.astype(f32), attention_bias.astype(f32), output_weight.astype(f32), output_bias.astype(f32), up_weight.astype(f32), up_bias.astype(f32), down_weight.astype(f32), down_bias.astype(f32))
    grads = backward(cotangent.astype(f32))
    return (outputs.astype(jnp.bfloat16), grads[0], grads[1], grads[2], grads[3], grads[4], grads[5], grads[6], grads[7], grads[8], grads[9], grads[10], grads[11])
```

```python
import functools
import math

import jax
import jax.numpy as jnp
from jax import lax
from jax.experimental import pallas as pl
from jax.experimental.pallas import tpu as pltpu
from jax.sharding import PartitionSpec as P

HD = 72


EPS = 1e-06
LOG2E = math.log2(math.e)
VMEM_LIMIT = 48 * 1024 * 1024
BOTH_LAST = (((1,), (1,)), ((), ()))
BOTH_FIRST = (((0,), (0,)), ((), ()))


def mm(a, b, dims=(((1,), (0,)), ((), ()))):
    return lax.dot_general(a, b, dims, preferred_element_type=jnp.float32)


def normalize(values):
    centred = values - jnp.mean(values, axis=-1, keepdims=True)
    inverse = lax.rsqrt(jnp.mean(centred * centred, axis=-1, keepdims=True) + EPS)
    return (centred * inverse, inverse)


def normalize_back(incoming, normed, inverse):
    first_mean = jnp.mean(incoming, axis=-1, keepdims=True)
    second_mean = jnp.mean(incoming * normed, axis=-1, keepdims=True)
    return inverse * (incoming - first_mean - normed * second_mean)


def modulate(normed, shift, scale):
    return (normed * (1.0 + scale) + shift).astype(jnp.bfloat16)


def silu_slope(values):
    sigmoid = jax.nn.sigmoid(values)
    return sigmoid * (1.0 + values * (1.0 - sigmoid))


def gelu_pair(values):
    root = math.sqrt(2.0 / math.pi)
    square = values * values
    bend = jnp.tanh(root * values * (1.0 + 0.044715 * square))
    half = 0.5 * (1.0 + bend)
    slope = half + 0.5 * values * (1.0 - bend * bend) * root * (1.0 + 3.0 * 0.044715 * square)
    return values * half, slope


def attend_kernel(start, packed_ref, out_ref, log_ref):
    rows, cols = out_ref.shape
    factor = LOG2E / math.sqrt(HD)
    pieces = []
    for head in range(cols // HD):
        at = head * HD
        queries = packed_ref[start : start + rows, at : at + HD]
        key_rows = packed_ref[:, cols + at : cols + at + HD]
        value_rows = packed_ref[:, 2 * cols + at : 2 * cols + at + HD]
        scores = mm(key_rows, queries, BOTH_LAST)
        top = jnp.max(scores, axis=0, keepdims=True)
        shares = jnp.exp2((scores - top) * factor)
        total = jnp.sum(shares, axis=0, keepdims=True)
        piece = mm(value_rows, shares.astype(jnp.bfloat16), BOTH_FIRST)
        pieces.append(piece / total)
        log_ref[head : head + 1, :] = top * factor + jnp.log2(total)
    out_ref[...] = jnp.concatenate(pieces, axis=0).T.astype(jnp.bfloat16)


def attend(packed, start, rows):
    length, width = packed.shape
    cols = width // 3
    heads = cols // HD
    return pl.pallas_call(
        functools.partial(attend_kernel, start),
        out_shape=(
            jax.ShapeDtypeStruct((rows, cols), jnp.bfloat16),
            jax.ShapeDtypeStruct((heads, rows), jnp.float32),
        ),
        in_specs=[pl.BlockSpec(memory_space=pltpu.VMEM)],
        out_specs=(pl.BlockSpec(memory_space=pltpu.VMEM),) * 2,
        compiler_params=pltpu.CompilerParams(vmem_limit_bytes=VMEM_LIMIT),
        cost_estimate=pl.CostEstimate(
            flops=4 * rows * length * 256 * heads,
            bytes_accessed=packed.size * 2 + rows * cols * 2,
            transcendentals=rows * length * heads,
        ),
    )(packed)


def attend_back_kernel(start, last, *refs):
    if last:
        packed_ref, up_ref, heads_ref, log_ref, key_in, value_in, query_ref, key_ref, value_ref = refs
    else:
        packed_ref, up_ref, heads_ref, log_ref, query_ref, key_ref, value_ref = refs
    rows, cols = up_ref.shape
    scale = 1.0 / math.sqrt(HD)
    factor = LOG2E * scale
    products = (up_ref[...].astype(jnp.float32) * heads_ref[...].astype(jnp.float32)).T
    pieces = []
    for head in range(cols // HD):
        at = head * HD
        here = slice(at, at + HD)
        queries = packed_ref[start : start + rows, at : at + HD]
        key_rows = packed_ref[:, cols + at : cols + at + HD]
        value_rows = packed_ref[:, 2 * cols + at : 2 * cols + at + HD]
        incoming = up_ref[:, here]
        inner = jnp.sum(products[here], axis=0, keepdims=True)
        scores = mm(key_rows, queries, BOTH_LAST)
        shares = jnp.exp2(scores * factor - log_ref[head : head + 1, :])
        grads = mm(value_rows, incoming, BOTH_LAST)
        score_grads = (shares * (grads - inner)).astype(jnp.bfloat16)
        value_grad = jnp.dot(shares.astype(jnp.bfloat16), incoming, preferred_element_type=jnp.float32)
        key_grad = jnp.dot(score_grads, queries, preferred_element_type=jnp.float32) * scale
        if last:
            value_grad += value_in[:, here]
            key_grad += key_in[:, here]
        value_ref[:, here] = value_grad.astype(value_ref.dtype)
        key_ref[:, here] = key_grad.astype(key_ref.dtype)
        pieces.append(mm(key_rows, score_grads, BOTH_FIRST) * scale)
    query_ref[...] = jnp.concatenate(pieces, axis=0).T.astype(jnp.bfloat16)


def attend_back(packed, start, upstream, heads_low, logs, sums, last):
    length, width = packed.shape
    cols = width // 3
    heads = cols // HD
    rows = upstream.shape[0]
    kind = jnp.bfloat16 if last else jnp.float32
    operands = (packed, upstream, heads_low, logs) + (sums if last else ())
    return pl.pallas_call(
        functools.partial(attend_back_kernel, start, last),
        out_shape=(
            jax.ShapeDtypeStruct((rows, cols), jnp.bfloat16),
            jax.ShapeDtypeStruct((length, cols), kind),
            jax.ShapeDtypeStruct((length, cols), kind),
        ),
        in_specs=[pl.BlockSpec(memory_space=pltpu.VMEM)] * len(operands),
        out_specs=(pl.BlockSpec(memory_space=pltpu.VMEM),) * 3,
        compiler_params=pltpu.CompilerParams(vmem_limit_bytes=VMEM_LIMIT),
        cost_estimate=pl.CostEstimate(
            flops=10 * rows * length * 256 * heads,
            bytes_accessed=packed.size * 2 + rows * cols * 6 + length * cols * 8,
            transcendentals=rows * length * heads,
        ),
    )(*operands)


def swap(values):
    return lax.ppermute(values, "tp", [(0, 1), (1, 0)])


def gather_rows(own, paired):
    if paired:
        return [own, swap(own)]
    return [lax.all_gather(own, "tp", axis=0, tiled=True)]


def scatter_rows(parts, paired):
    if paired:
        return parts[0] + swap(parts[1].astype(jnp.bfloat16)).astype(jnp.float32)
    whole = jnp.concatenate(parts, axis=0).astype(jnp.bfloat16)
    return lax.psum_scatter(whole, "tp", scatter_dimension=0, tiled=True).astype(jnp.float32)


def gather_columns(own):
    if lax.axis_size("tp") == 2:
        other = swap(own)
        left = lax.axis_index("tp") == 0
        return jnp.concatenate([jnp.where(left, own, other), jnp.where(left, other, own)], axis=-1)
    return lax.all_gather(own, "tp", axis=own.ndim - 1, tiled=True)


def scatter_columns(whole):
    count = lax.axis_size("tp")
    if count == 2:
        width = whole.shape[-1] // 2
        left = lax.axis_index("tp") == 0
        halves = whole[..., :width], whole[..., width:]
        own = jnp.where(left, halves[0], halves[1])
        return own + swap(jnp.where(left, halves[1], halves[0]))
    return lax.psum_scatter(whole, "tp", scatter_dimension=whole.ndim - 1, tiled=True)


def sum_pair(values):
    if lax.axis_size("tp") == 2:
        return values + swap(values)
    return lax.psum(values, "tp")


def exchange(blocks):
    return lax.all_to_all(blocks, "fsdp", 0, 0, tiled=True)


def share(values):
    return exchange(jnp.broadcast_to(values[None], (lax.axis_size("fsdp"),) + values.shape))


def per_device(
    inputs,
    conditions,
    modulation_weight,
    modulation_bias,
    attention_weight,
    attention_bias,
    output_weight,
    output_bias,
    up_weight,
    up_bias,
    down_weight,
    down_bias,
    cotangent,
):
    tp = lax.axis_size("tp")
    rank = lax.axis_index("tp")
    fsdp = lax.axis_size("fsdp")
    local_rows, width = inputs.shape
    latents = conditions.shape[0]
    length = local_rows * tp // latents
    depth = attention_weight.shape[0]
    cols = attention_weight.shape[2]
    hidden = up_weight.shape[1]
    paired = tp == 2 and latents == 1
    f32 = jnp.float32
    bf16 = jnp.bfloat16

    first_shard = jnp.concatenate([attention_weight.reshape(depth, 3 * cols), output_weight.T], axis=1)
    first_weights = lax.all_gather(first_shard, "fsdp", axis=0, tiled=True)
    up_all = lax.all_gather(up_weight, "fsdp", axis=0, tiled=True)
    down_all = lax.all_gather(down_weight.T, "fsdp", axis=0, tiled=True)
    attention_all = first_weights[:, : 3 * cols]
    output_all = first_weights[:, 3 * cols :]

    condition_values = conditions.astype(f32)
    silu_low = jax.nn.silu(condition_values).astype(bf16)
    silu_rows = exchange(silu_low.reshape(latents, fsdp, depth).transpose(1, 0, 2))
    silu_rows = silu_rows.reshape(fsdp * latents, depth)
    modulation_flat = modulation_weight.reshape(depth, 6 * cols)
    partial = mm(silu_rows, modulation_flat).reshape(fsdp, latents, 6 * cols)
    own_columns = jnp.sum(exchange(partial), axis=0).reshape(latents, 6, cols)
    modulation = gather_columns(own_columns + modulation_bias.astype(f32))
    own_modulation = modulation[0]
    if latents > 1:
        own_modulation = lax.dynamic_index_in_dim(
            modulation, rank * local_rows // length, 0, keepdims=False
        )

    def own_rows(group):
        return own_modulation[group][None]

    def all_rows(group):
        if latents == 1:
            return modulation[0, group][None]
        return jnp.repeat(modulation[:, group], length, axis=0)

    def sum_latents(values):
        return jnp.sum(values.reshape(latents, length, width), axis=1)

    def place_latent(values):
        total = jnp.sum(values, axis=0)[None]
        if latents == 1:
            return total
        mine = jnp.arange(latents)[:, None] == rank * local_rows // length
        return jnp.where(mine, total, 0.0)

    inputs_all = jnp.concatenate(gather_rows(inputs, paired), axis=0)
    cotangent_parts = gather_rows(cotangent, paired)
    input_values = inputs.astype(f32)
    first_normed, first_inverse = normalize(input_values)
    first_normed_all, _ = normalize(inputs_all.astype(f32))
    first_all = modulate(first_normed_all, all_rows(0), all_rows(1))
    bias_rows = attention_bias.astype(f32)
    packed_bias = jnp.concatenate([bias_rows[0], jnp.zeros((cols,), f32), bias_rows[1]])
    packed = (mm(first_all, attention_all) + packed_bias).astype(bf16)

    block = local_rows
    blocks = length // block
    group_blocks = latents * blocks
    packed_latents = [packed[n * length : (n + 1) * length] for n in range(latents)]
    heads_parts = [None] * group_blocks
    logs = [None] * group_blocks
    products = [None] * group_blocks
    for at in reversed(range(group_blocks)):
        latent, start = at // blocks, at % blocks * block
        heads_parts[at], logs[at] = attend(packed_latents[latent], start, block)
        products[at] = mm(heads_parts[at], output_all, BOTH_LAST)
    attention = scatter_rows(products, paired) + output_bias.astype(f32)
    mid = input_values + own_rows(2) * attention
    second_normed, second_inverse = normalize(mid)
    second_parts = gather_rows(modulate(second_normed, own_rows(3), own_rows(4)), paired)

    gate_all = all_rows(5)
    if paired:
        feed_parts = [(gate_all * part.astype(f32)).astype(bf16) for part in cotangent_parts]
    else:
        feed_parts = [(gate_all * cotangent_parts[0].astype(f32)).astype(bf16)]
    up_bias_row = up_bias.astype(f32)[None]
    act_parts = []
    pre_parts = []
    for second, feed_grad in zip(second_parts, feed_parts):
        act, slope = gelu_pair(mm(second, up_all) + up_bias_row)
        act_parts.append(act.astype(bf16))
        pre_parts.append((mm(feed_grad, down_all) * slope).astype(bf16))
    second_grad = scatter_rows([mm(part, up_all, BOTH_LAST) for part in pre_parts], paired)
    feed = scatter_rows([mm(part, down_all, BOTH_LAST) for part in act_parts], paired)
    feed = feed + down_bias.astype(f32)
    outputs = (mid + own_rows(5) * feed).astype(bf16)

    feed_all = jnp.concatenate(feed_parts, axis=0)
    act_all = jnp.concatenate(act_parts, axis=0)
    pre_all = jnp.concatenate(pre_parts, axis=0)
    second_all = jnp.concatenate(second_parts, axis=0)

    def scatter_weights(values):
        return lax.psum_scatter(
            values.astype(bf16), "fsdp", scatter_dimension=0, tiled=True
        ).astype(f32)

    grad_down = scatter_weights(mm(feed_all, act_all, BOTH_FIRST))
    grad_up_weight = scatter_weights(mm(second_all, pre_all, BOTH_FIRST))

    upstream = cotangent.astype(f32)
    mid_grad = upstream + normalize_back(
        second_grad * (1.0 + own_rows(4)), second_normed, second_inverse
    )
    attention_low = (own_rows(2) * mid_grad).astype(bf16)
    upstream_parts = gather_rows(attention_low, paired)
    if paired:
        heads_grads = [mm(part, output_all).astype(bf16) for part in upstream_parts]
    else:
        heads_grad = mm(upstream_parts[0], output_all).astype(bf16)
        heads_grads = [heads_grad[n * block : (n + 1) * block] for n in range(group_blocks)]
    query_grads = []
    key_grads = []
    value_grads = []
    for latent in range(latents):
        sums = ()
        for step in range(blocks):
            at = latent * blocks + step
            query_grad, *sums = attend_back(
                packed_latents[latent],
                step * block,
                heads_grads[at],
                heads_parts[at],
                logs[at],
                tuple(sums),
                step == blocks - 1,
            )
            query_grads.append(query_grad)
        key_grads.append(sums[0])
        value_grads.append(sums[1])
    packed_low = jnp.concatenate(
        [jnp.concatenate(part, axis=0) for part in (query_grads, key_grads, value_grads)], axis=1
    )
    first_grad_all = mm(packed_low, attention_all, BOTH_LAST)
    attention_grad = mm(first_all, packed_low, BOTH_FIRST)
    output_grad = mm(
        jnp.concatenate(upstream_parts, axis=0), jnp.concatenate(heads_parts, axis=0), BOTH_FIRST
    )
    first_grads = scatter_weights(jnp.concatenate([attention_grad, output_grad], axis=1))

    if paired:
        first_grad_parts = [first_grad_all[:local_rows], first_grad_all[local_rows:]]
    else:
        first_grad_parts = [first_grad_all]
    first_grad = scatter_rows(first_grad_parts, paired)
    grad_inputs = mid_grad + normalize_back(
        first_grad * (1.0 + own_rows(1)), first_normed, first_inverse
    )

    modulation_parts = jnp.stack(
        [
            sum_latents(first_grad_all),
            sum_latents(first_grad_all * first_normed_all),
            place_latent(mid_grad * attention),
            place_latent(second_grad),
            place_latent(second_grad * second_normed),
            place_latent(upstream * feed),
        ],
        axis=1,
    )
    modulation_low = scatter_columns(modulation_parts).astype(bf16)
    modulation_all = share(modulation_low.reshape(latents, 6 * cols)).reshape(
        fsdp * latents, 6 * cols
    )
    grad_modulation_weight = mm(silu_rows, modulation_all, BOTH_FIRST).reshape(depth, 6, cols)
    grad_modulation_bias = jnp.sum(modulation_all, axis=0, dtype=f32).reshape(6, cols)
    silu_part = sum_pair(mm(modulation_all, modulation_flat, BOTH_LAST))
    silu_total = exchange(silu_part.reshape(fsdp, latents, depth))
    silu_total = silu_total.transpose(1, 0, 2).reshape(latents, width)
    grad_conditions = silu_total * silu_slope(condition_values)

    own_feed = feed_parts[0]
    if not paired:
        own_feed = (own_rows(5) * upstream).astype(bf16)
    token_sums = sum_pair(
        jnp.concatenate(
            [
                jnp.sum(attention_low, axis=0, dtype=f32),
                jnp.sum(own_feed, axis=0, dtype=f32),
            ]
        )
    )
    bias_parts = jnp.concatenate(
        [
            token_sums,
            jnp.sum(packed_low, axis=0, dtype=f32),
            jnp.sum(pre_all, axis=0, dtype=f32),
        ]
    )
    bias_sums = jnp.sum(share(bias_parts), axis=0)
    grad_output_bias = bias_sums[:width]
    grad_down_bias = bias_sums[width : 2 * width]
    packed_sums = bias_sums[2 * width : 2 * width + 3 * cols]
    grad_attention_bias = jnp.stack([packed_sums[:cols], packed_sums[2 * cols :]])
    grad_up_bias = bias_sums[2 * width + 3 * cols :]
    return (
        outputs,
        grad_inputs,
        grad_conditions,
        grad_modulation_weight,
        grad_modulation_bias,
        first_grads[:, : 3 * cols].reshape(depth, 3, cols),
        grad_attention_bias,
        first_grads[:, 3 * cols :].T,
        grad_output_bias,
        grad_up_weight,
        grad_up_bias,
        grad_down.T,
        grad_down_bias,
    )


def solution(mesh):
    placed = (
        P(("fsdp", "tp"), None),
        P("fsdp", None),
        P("fsdp", None, "tp"),
        P(None, "tp"),
        P("fsdp", None, "tp"),
        P(None, "tp"),
        P("tp", "fsdp"),
        P(),
        P("fsdp", "tp"),
        P("tp"),
        P("tp", "fsdp"),
        P(),
        P(("fsdp", "tp"), None),
    )
    return jax.shard_map(
        per_device,
        mesh=mesh,
        in_specs=placed,
        out_specs=(
            P(("fsdp", "tp"), None),
            P(("fsdp", "tp"), None),
            P("fsdp", None),
            P("fsdp", None, "tp"),
            P(None, "tp"),
            P("fsdp", None, "tp"),
            P(None, "tp"),
            P("tp", "fsdp"),
            P(),
            P("fsdp", "tp"),
            P("tp"),
            P("tp", "fsdp"),
            P(),
        ),
        check_vma=False,
    )
```

```python
import functools
import math

import jax
import jax.numpy as jnp
from jax import lax
from jax.experimental import pallas as pl
from jax.experimental.pallas import tpu as pltpu
from jax.sharding import PartitionSpec as P

HD = 72


EPS = 1e-06
LOG2E = math.log2(math.e)
VMEM_LIMIT = 48 * 1024 * 1024
TILE = 768
BOTH_LAST = (((1,), (1,)), ((), ()))
BOTH_FIRST = (((0,), (0,)), ((), ()))


def mm(a, b, dims=(((1,), (0,)), ((), ()))):
    return lax.dot_general(a, b, dims, preferred_element_type=jnp.float32)


def normalize(values):
    centred = values - jnp.mean(values, axis=-1, keepdims=True)
    inverse = lax.rsqrt(jnp.mean(centred * centred, axis=-1, keepdims=True) + EPS)
    return (centred * inverse, inverse)


def normalize_back(incoming, normed, inverse):
    first_mean = jnp.mean(incoming, axis=-1, keepdims=True)
    second_mean = jnp.mean(incoming * normed, axis=-1, keepdims=True)
    return inverse * (incoming - first_mean - normed * second_mean)


def modulate(normed, shift, scale):
    return (normed * (1.0 + scale) + shift).astype(jnp.bfloat16)


def silu_slope(values):
    sigmoid = jax.nn.sigmoid(values)
    return sigmoid * (1.0 + values * (1.0 - sigmoid))


def gelu_pair(values):
    root = math.sqrt(2.0 / math.pi)
    square = values * values
    bend = jnp.tanh(root * values * (1.0 + 0.044715 * square))
    half = 0.5 * (1.0 + bend)
    slope = half + 0.5 * values * (1.0 - bend * bend) * root * (1.0 + 3.0 * 0.044715 * square)
    return values * half, slope


def attend_kernel(start, packed_ref, out_ref, log_ref):
    rows, cols = out_ref.shape
    factor = LOG2E / math.sqrt(HD)
    pieces = []
    for head in range(cols // HD):
        at = head * HD
        queries = packed_ref[start : start + rows, at : at + HD]
        key_rows = packed_ref[:, cols + at : cols + at + HD]
        value_rows = packed_ref[:, 2 * cols + at : 2 * cols + at + HD]
        scores = mm(key_rows, queries, BOTH_LAST)
        top = jnp.max(scores, axis=0, keepdims=True)
        shares = jnp.exp2((scores - top) * factor)
        total = jnp.sum(shares, axis=0, keepdims=True)
        piece = mm(value_rows, shares.astype(jnp.bfloat16), BOTH_FIRST)
        pieces.append(piece / total)
        log_ref[head : head + 1, :] = top * factor + jnp.log2(total)
    out_ref[...] = jnp.concatenate(pieces, axis=0).T.astype(jnp.bfloat16)


def attend(packed, start, rows):
    length, width = packed.shape
    cols = width // 3
    heads = cols // HD
    return pl.pallas_call(
        functools.partial(attend_kernel, start),
        out_shape=(
            jax.ShapeDtypeStruct((rows, cols), jnp.bfloat16),
            jax.ShapeDtypeStruct((heads, rows), jnp.float32),
        ),
        in_specs=[pl.BlockSpec(memory_space=pltpu.VMEM)],
        out_specs=(pl.BlockSpec(memory_space=pltpu.VMEM),) * 2,
        compiler_params=pltpu.CompilerParams(vmem_limit_bytes=VMEM_LIMIT),
        cost_estimate=pl.CostEstimate(
            flops=4 * rows * length * 256 * heads,
            bytes_accessed=packed.size * 2 + rows * cols * 2,
            transcendentals=rows * length * heads,
        ),
    )(packed)


def attend_back_kernel(start, last, *refs):
    packed_ref, up_ref, heads_ref, log_ref = refs[:4]
    rows, cols = up_ref.shape
    if last:
        query_ins, key_in, value_in, out_ref, sum_ref = refs[4:-4], *refs[-4:]
    else:
        query_ref, key_ref, value_ref = refs[4:]
    scale = 1.0 / math.sqrt(HD)
    factor = LOG2E * scale
    products = (up_ref[...].astype(jnp.float32) * heads_ref[...].astype(jnp.float32)).T
    pieces = []
    for head in range(cols // HD):
        at = head * HD
        here = slice(at, at + HD)
        queries = packed_ref[start : start + rows, at : at + HD]
        key_rows = packed_ref[:, cols + at : cols + at + HD]
        value_rows = packed_ref[:, 2 * cols + at : 2 * cols + at + HD]
        incoming = up_ref[:, here]
        inner = jnp.sum(products[here], axis=0, keepdims=True)
        scores = mm(key_rows, queries, BOTH_LAST)
        shares = jnp.exp2(scores * factor - log_ref[head : head + 1, :])
        grads = mm(value_rows, incoming, BOTH_LAST)
        score_grads = (shares * (grads - inner)).astype(jnp.bfloat16)
        value_grad = jnp.dot(shares.astype(jnp.bfloat16), incoming, preferred_element_type=jnp.float32)
        key_grad = jnp.dot(score_grads, queries, preferred_element_type=jnp.float32) * scale
        if last:
            value_grad += value_in[:, here]
            key_grad += key_in[:, here]
            out_ref[:, 2 * cols + at : 2 * cols + at + HD] = value_grad.astype(jnp.bfloat16)
            out_ref[:, cols + at : cols + at + HD] = key_grad.astype(jnp.bfloat16)
        else:
            value_ref[:, here] = value_grad
            key_ref[:, here] = key_grad
        pieces.append(mm(key_rows, score_grads, BOTH_FIRST) * scale)
    query_grad = jnp.concatenate(pieces, axis=0).T.astype(jnp.bfloat16)
    if last:
        for step, query_in in enumerate(query_ins):
            out_ref[step * rows : (step + 1) * rows, :cols] = query_in[...]
        out_ref[start : start + rows, :cols] = query_grad
        sum_ref[...] = jnp.sum(out_ref[...].astype(jnp.float32), axis=0, keepdims=True)
    else:
        query_ref[...] = query_grad


def attend_back(packed, start, upstream, heads_low, logs, query_grads, sums, last):
    length, width = packed.shape
    cols = width // 3
    heads = cols // HD
    rows = upstream.shape[0]
    operands = (packed, upstream, heads_low, logs)
    if last:
        operands += tuple(query_grads) + tuple(sums)
        shapes = (
            jax.ShapeDtypeStruct((length, width), jnp.bfloat16),
            jax.ShapeDtypeStruct((1, width), jnp.float32),
        )
    else:
        shapes = (
            jax.ShapeDtypeStruct((rows, cols), jnp.bfloat16),
            jax.ShapeDtypeStruct((length, cols), jnp.float32),
            jax.ShapeDtypeStruct((length, cols), jnp.float32),
        )
    return pl.pallas_call(
        functools.partial(attend_back_kernel, start, last),
        out_shape=shapes,
        in_specs=[pl.BlockSpec(memory_space=pltpu.VMEM)] * len(operands),
        out_specs=jax.tree.map(lambda _: pl.BlockSpec(memory_space=pltpu.VMEM), shapes),
        compiler_params=pltpu.CompilerParams(vmem_limit_bytes=VMEM_LIMIT),
        cost_estimate=pl.CostEstimate(
            flops=10 * rows * length * 256 * heads,
            bytes_accessed=packed.size * 2 + rows * cols * 6 + length * cols * 8,
            transcendentals=rows * length * heads,
        ),
    )(*operands)


def feed_kernel(second_ref, feed_ref, up_ref, down_ref, bias_ref, act_ref, pre_ref, sum_ref):
    act, slope = gelu_pair(mm(second_ref[...], up_ref[...]) + bias_ref[...])
    act_ref[...] = act.astype(jnp.bfloat16)
    low = (mm(feed_ref[...], down_ref[...]) * slope).astype(jnp.bfloat16)
    pre_ref[...] = low
    sum_ref[...] = jnp.sum(low.astype(jnp.float32), axis=0, keepdims=True)


def feed_forward(second, feed_grad, weights, bias):
    rows, width = second.shape
    hidden = weights.shape[1] // 2
    tile = TILE
    tiles = hidden // tile
    if hidden % tile:
        act, slope = gelu_pair(mm(second, weights[:, :hidden]) + bias)
        low = (mm(feed_grad, weights[:, hidden:]) * slope).astype(jnp.bfloat16)
        sums = jnp.sum(low, axis=0, keepdims=True, dtype=jnp.float32)
        return act.astype(jnp.bfloat16), low, sums
    whole = pl.BlockSpec((rows, width), lambda j: (0, 0))
    piece = pl.BlockSpec((rows, tile), lambda j: (0, j))
    line = pl.BlockSpec((1, tile), lambda j: (0, j))
    return pl.pallas_call(
        feed_kernel,
        grid=(tiles,),
        out_shape=(
            jax.ShapeDtypeStruct((rows, hidden), jnp.bfloat16),
            jax.ShapeDtypeStruct((rows, hidden), jnp.bfloat16),
            jax.ShapeDtypeStruct((1, hidden), jnp.float32),
        ),
        in_specs=[
            whole,
            whole,
            pl.BlockSpec((width, tile), lambda j: (0, j)),
            pl.BlockSpec((width, tile), lambda j: (0, j + tiles)),
            line,
        ],
        out_specs=(piece, piece, line),
        compiler_params=pltpu.CompilerParams(vmem_limit_bytes=VMEM_LIMIT),
        cost_estimate=pl.CostEstimate(
            flops=4 * rows * width * hidden,
            bytes_accessed=2 * (2 * second.size + weights.size + 2 * rows * hidden),
            transcendentals=rows * hidden,
        ),
    )(second, feed_grad, weights, weights, bias)


def feed_weight_kernel(tiles, feed_ref, second_ref, act_ref, pre_ref, out_ref, turned_ref):
    step = pl.program_id(0)

    @pl.when(step == 0)
    def _():
        turned_ref[...] = feed_ref[...].T

    @pl.when(step == tiles)
    def _():
        turned_ref[...] = second_ref[...].T

    @pl.when(step < tiles)
    def _():
        out_ref[...] = mm(turned_ref[...], act_ref[...]).astype(jnp.bfloat16)

    @pl.when(step >= tiles)
    def _():
        out_ref[...] = mm(turned_ref[...], pre_ref[...]).astype(jnp.bfloat16)


def feed_weight_grads(feed_grad, second, act, pre):
    rows, width = second.shape
    hidden = act.shape[1]
    tile = TILE
    tiles = hidden // tile
    if hidden % tile:
        grads = [mm(feed_grad, act, BOTH_FIRST), mm(second, pre, BOTH_FIRST)]
        return jnp.concatenate(grads, axis=1).astype(jnp.bfloat16)
    whole = pl.BlockSpec((rows, width), lambda j: (0, 0))
    return pl.pallas_call(
        functools.partial(feed_weight_kernel, tiles),
        grid=(2 * tiles,),
        out_shape=jax.ShapeDtypeStruct((width, 2 * hidden), jnp.bfloat16),
        in_specs=[
            whole,
            whole,
            pl.BlockSpec((rows, tile), lambda j: (0, jnp.minimum(j, tiles - 1))),
            pl.BlockSpec((rows, tile), lambda j: (0, jnp.maximum(j - tiles, 0))),
        ],
        out_specs=pl.BlockSpec((width, tile), lambda j: (0, j)),
        scratch_shapes=[pltpu.VMEM((width, rows), jnp.bfloat16)],
        compiler_params=pltpu.CompilerParams(vmem_limit_bytes=VMEM_LIMIT),
        cost_estimate=pl.CostEstimate(
            flops=4 * rows * width * hidden,
            bytes_accessed=4 * (second.size + act.size + width * hidden),
            transcendentals=0,
        ),
    )(feed_grad, second, act, pre)


def weight_kernel(first_ref, packed_ref, upstream_ref, heads_ref, out_ref):
    width, wide = out_ref.shape
    cut = packed_ref.shape[1]
    step = width // 3

    def body(index, carry):
        rows = pl.ds(pl.multiple_of(index * step, step), step)
        out_ref[rows, :cut] = mm(first_ref[:, rows], packed_ref[...], BOTH_FIRST).astype(jnp.bfloat16)
        out_ref[rows, cut:] = mm(upstream_ref[:, rows], heads_ref[...], BOTH_FIRST).astype(jnp.bfloat16)
        return carry

    lax.fori_loop(0, width // step, body, 0)


def weight_grads(first, packed, upstream, heads):
    width = first.shape[1]
    wide = packed.shape[1] + heads.shape[1]
    return pl.pallas_call(
        weight_kernel,
        out_shape=jax.ShapeDtypeStruct((width, wide), jnp.bfloat16),
        in_specs=[pl.BlockSpec(memory_space=pltpu.VMEM)] * 4,
        out_specs=pl.BlockSpec(memory_space=pltpu.VMEM),
        compiler_params=pltpu.CompilerParams(vmem_limit_bytes=VMEM_LIMIT),
        cost_estimate=pl.CostEstimate(
            flops=2 * first.shape[0] * width * wide,
            bytes_accessed=2 * (first.size + packed.size + upstream.size + heads.size + width * wide),
            transcendentals=0,
        ),
    )(first, packed, upstream, heads)


def swap(values):
    return lax.ppermute(values, "tp", [(0, 1), (1, 0)])


def gather_rows(own, paired):
    if paired:
        return [own, swap(own)]
    return [lax.all_gather(own, "tp", axis=0, tiled=True)]


def scatter_rows(parts, paired):
    if paired:
        return parts[0] + swap(parts[1].astype(jnp.bfloat16)).astype(jnp.float32)
    whole = jnp.concatenate(parts, axis=0).astype(jnp.bfloat16)
    return lax.psum_scatter(whole, "tp", scatter_dimension=0, tiled=True).astype(jnp.float32)


def gather_columns(own):
    if lax.axis_size("tp") == 2:
        other = swap(own)
        left = lax.axis_index("tp") == 0
        return jnp.concatenate([jnp.where(left, own, other), jnp.where(left, other, own)], axis=-1)
    return lax.all_gather(own, "tp", axis=own.ndim - 1, tiled=True)


def take_columns(whole):
    count = lax.axis_size("tp")
    piece = whole.shape[1] // count
    if count == 2:
        return jnp.where(lax.axis_index("tp") == 0, whole[:, :piece], whole[:, piece:])
    return lax.dynamic_slice_in_dim(whole, lax.axis_index("tp") * piece, piece, 1)


def sum_pair(values):
    if lax.axis_size("tp") == 2:
        return values + swap(values)
    return lax.psum(values, "tp")


def exchange(blocks):
    return lax.all_to_all(blocks, "fsdp", 0, 0, tiled=True)


def share(values):
    return exchange(jnp.broadcast_to(values[None], (lax.axis_size("fsdp"),) + values.shape))


def hop(values, z_step, x_step, core_step):
    planes = lax.axis_size("fsdp") // 4
    moves = []
    for source in range(4 * planes):
        z, x, core = source // 4, source // 2 % 2, source % 2
        target = ((z + z_step) % planes * 2 + (x + x_step) % 2) * 2 + (core + core_step) % 2
        moves.append((source, target))
    return lax.ppermute(values, "fsdp", moves)


def place():
    index = lax.axis_index("fsdp")
    return index // 4, index // 2 % 2, index % 2


def per_device(
    inputs,
    conditions,
    modulation_weight,
    modulation_bias,
    attention_weight,
    attention_bias,
    output_weight,
    output_bias,
    up_weight,
    up_bias,
    down_weight,
    down_bias,
    cotangent,
):
    tp = lax.axis_size("tp")
    rank = lax.axis_index("tp")
    fsdp = lax.axis_size("fsdp")
    local_rows, width = inputs.shape
    latents = conditions.shape[0]
    length = local_rows * tp // latents
    depth = attention_weight.shape[0]
    cols = attention_weight.shape[2]
    hidden = up_weight.shape[1]
    paired = tp == 2 and latents == 1
    f32 = jnp.float32
    bf16 = jnp.bfloat16

    first_shard = jnp.concatenate([attention_weight.reshape(depth, 3 * cols), output_weight.T], axis=1)
    first_weights = lax.all_gather(first_shard, "fsdp", axis=0, tiled=True)
    attention_all = first_weights[:, : 3 * cols]
    output_all = first_weights[:, 3 * cols :]
    feed_shard = jnp.concatenate([up_weight, down_weight.T], axis=1)

    inputs_parts = gather_rows(inputs, paired)

    condition_values = conditions.astype(f32)
    silu_low = jax.nn.silu(condition_values).astype(bf16)
    silu_rows = exchange(silu_low.reshape(latents, fsdp, depth).transpose(1, 0, 2))
    silu_rows = silu_rows.reshape(fsdp * latents, depth)
    modulation_flat = modulation_weight.reshape(depth, 6 * cols)
    partial = mm(silu_rows, modulation_flat).reshape(fsdp, latents, 6 * cols)
    own_columns = jnp.sum(exchange(partial), axis=0).reshape(latents, 6, cols)
    own_columns, inputs_parts = lax.optimization_barrier((own_columns, inputs_parts))
    modulation = gather_columns(own_columns + modulation_bias.astype(f32))
    feed_shard, modulation = lax.optimization_barrier((feed_shard, modulation))
    feed_weights = lax.all_gather(feed_shard, "fsdp", axis=0, tiled=True)
    up_all = feed_weights[:, :hidden]
    down_all = feed_weights[:, hidden:]
    own_modulation = modulation[0]
    if latents > 1:
        own_modulation = lax.dynamic_index_in_dim(
            modulation, rank * local_rows // length, 0, keepdims=False
        )

    def own_rows(group):
        return own_modulation[group][None]

    def all_rows(group):
        if latents == 1:
            return modulation[0, group][None]
        return jnp.repeat(modulation[:, group], length, axis=0)

    def sum_latents(values):
        return jnp.sum(values.reshape(latents, length, width), axis=1)

    def place_latent(values):
        total = jnp.sum(values, axis=0)[None]
        if latents == 1:
            return total
        mine = jnp.arange(latents)[:, None] == rank * local_rows // length
        return jnp.where(mine, total, 0.0)

    cotangent_late, inputs_parts = lax.optimization_barrier((cotangent, inputs_parts))
    inputs_all = jnp.concatenate(inputs_parts, axis=0)
    cotangent_parts = gather_rows(cotangent_late, paired)
    input_values = inputs.astype(f32)
    first_normed, first_inverse = normalize(input_values)
    first_normed_all, _ = normalize(inputs_all.astype(f32))
    first_all = modulate(first_normed_all, all_rows(0), all_rows(1))
    bias_rows = attention_bias.astype(f32)
    packed_bias = jnp.concatenate([bias_rows[0], jnp.zeros((cols,), f32), bias_rows[1]])
    packed = (mm(first_all, attention_all) + packed_bias).astype(bf16)
    packed, cotangent_parts = lax.optimization_barrier((packed, cotangent_parts))

    block = local_rows
    blocks = length // block
    group_blocks = latents * blocks
    packed_latents = [packed[n * length : (n + 1) * length] for n in range(latents)]
    heads_parts = [None] * group_blocks
    logs = [None] * group_blocks
    products = [None] * group_blocks
    for at in reversed(range(group_blocks)):
        latent, start = at // blocks, at % blocks * block
        heads_parts[at], logs[at] = attend(packed_latents[latent], start, block)
        products[at] = mm(heads_parts[at], output_all, BOTH_LAST)
    attention = scatter_rows(products, paired) + output_bias.astype(f32)
    mid = input_values + own_rows(2) * attention
    second_normed, second_inverse = normalize(mid)
    second_parts = gather_rows(modulate(second_normed, own_rows(3), own_rows(4)), paired)

    gate_all = all_rows(5)
    if paired:
        feed_parts = [(gate_all * part.astype(f32)).astype(bf16) for part in cotangent_parts]
    else:
        feed_parts = [(gate_all * cotangent_parts[0].astype(f32)).astype(bf16)]
    feed_all = jnp.concatenate(feed_parts, axis=0)
    second_all = jnp.concatenate(second_parts, axis=0)
    act_all, pre_all, pre_sum = feed_forward(
        second_all, feed_all, feed_weights, up_bias.astype(f32)[None]
    )
    feed_grads = feed_weight_grads(feed_all, second_all, act_all, pre_all)

    def scatter_weights(values):
        return lax.psum_scatter(
            values.astype(bf16), "fsdp", scatter_dimension=0, tiled=True
        ).astype(f32)

    feed_grads, act_all, pre_all = lax.optimization_barrier((feed_grads, act_all, pre_all))
    feed_grads = scatter_weights(feed_grads)
    rows_kept = local_rows if paired else local_rows * tp
    act_parts = [act_all[:rows_kept], act_all[rows_kept:]][: len(second_parts)]
    pre_parts = [pre_all[:rows_kept], pre_all[rows_kept:]][: len(second_parts)]
    feed_sums = [mm(part, down_all, BOTH_LAST) for part in act_parts]
    second_sums = [mm(part, up_all, BOTH_LAST) for part in pre_parts]

    second_grad = scatter_rows(second_sums, paired)
    upstream = cotangent.astype(f32)
    mid_grad = upstream + normalize_back(
        second_grad * (1.0 + own_rows(4)), second_normed, second_inverse
    )
    attention_low = (own_rows(2) * mid_grad).astype(bf16)
    upstream_parts = gather_rows(attention_low, paired)
    if paired:
        feed_sums[1] = feed_sums[1].astype(bf16)
        feed_sums[1], upstream_parts[1] = lax.optimization_barrier((feed_sums[1], upstream_parts[1]))
    feed = scatter_rows(feed_sums, paired) + down_bias.astype(f32)
    if paired:
        heads_grads = [mm(part, output_all).astype(bf16) for part in upstream_parts]
    else:
        heads_grad = mm(upstream_parts[0], output_all).astype(bf16)
        heads_grads = [heads_grad[n * block : (n + 1) * block] for n in range(group_blocks)]
    packed_parts = []
    packed_sums = []
    for latent in range(latents):
        query_grads = []
        sums = (jnp.zeros((length, cols), f32),) * 2
        for step in range(blocks):
            at = latent * blocks + step
            result = attend_back(
                packed_latents[latent],
                step * block,
                heads_grads[at],
                heads_parts[at],
                logs[at],
                query_grads,
                sums,
                step == blocks - 1,
            )
            if step < blocks - 1:
                query_grads.append(result[0])
                sums = result[1:] if step == 0 else tuple(map(jnp.add, sums, result[1:]))
        packed_parts.append(result[0])
        packed_sums.append(result[1])
    packed_low = packed_parts[0] if latents == 1 else jnp.concatenate(packed_parts, axis=0)
    packed_sum = jnp.sum(jnp.concatenate(packed_sums, axis=0), axis=0)
    first_grads = weight_grads(
        first_all,
        packed_low,
        jnp.concatenate(upstream_parts, axis=0),
        jnp.concatenate(heads_parts, axis=0),
    )
    first_grads, feed, packed_low = lax.optimization_barrier((first_grads, feed, packed_low))
    first_grads, feed_grads = lax.optimization_barrier((first_grads, feed_grads))
    first_grads = scatter_weights(first_grads)
    grad_attention = first_grads[:, : 3 * cols]
    grad_output = first_grads[:, 3 * cols :].T
    outputs = (mid + own_rows(5) * feed).astype(bf16)
    first_grad_all = mm(packed_low, attention_all, BOTH_LAST)

    own_feed = feed_parts[0]
    if not paired:
        own_feed = (own_rows(5) * upstream).astype(bf16)
    token_sums = jnp.stack(
        [
            sum_latents(first_grad_all),
            sum_latents(first_grad_all * first_normed_all),
            place_latent(mid_grad * attention),
            place_latent(second_grad),
            place_latent(second_grad * second_normed),
            place_latent(upstream * feed),
        ],
        axis=1,
    )
    token_sums = jnp.concatenate(
        [
            token_sums.reshape(latents * 6, width),
            jnp.sum(attention_low, axis=0, dtype=f32, keepdims=True),
            jnp.sum(own_feed, axis=0, dtype=f32, keepdims=True),
        ]
    )
    token_sums = sum_pair(token_sums)
    first_grad_all, token_sums = lax.optimization_barrier((first_grad_all, token_sums))
    if paired:
        first_grad_parts = [first_grad_all[:local_rows], first_grad_all[local_rows:]]
    else:
        first_grad_parts = [first_grad_all]
    first_grad = scatter_rows(first_grad_parts, paired)
    modulation_low = take_columns(token_sums[: latents * 6]).astype(bf16)
    sums = jnp.concatenate(
        [
            modulation_low.astype(f32).reshape(latents * 6 * cols),
            token_sums[latents * 6 :].reshape(2 * width),
            packed_sum,
            pre_sum[0],
        ]
    )
    shared = share(sums[None]).reshape(fsdp, -1)
    shared, first_grad = lax.optimization_barrier((shared, first_grad))
    modulation_all = shared[:, : latents * 6 * cols].reshape(fsdp * latents, 6 * cols).astype(bf16)
    bias_sums = jnp.sum(shared[:, latents * 6 * cols :], axis=0)
    grad_modulation_weight = mm(silu_rows, modulation_all, BOTH_FIRST).reshape(depth, 6, cols)
    grad_modulation_bias = jnp.sum(modulation_all, axis=0, dtype=f32).reshape(6, cols)
    silu_part = sum_pair(mm(modulation_all, modulation_flat, BOTH_LAST))
    silu_total = exchange(silu_part.reshape(fsdp, latents, depth))
    silu_total = silu_total.transpose(1, 0, 2).reshape(latents, width)
    grad_inputs = mid_grad + normalize_back(
        first_grad * (1.0 + own_rows(1)), first_normed, first_inverse
    )
    grad_conditions = silu_total * silu_slope(condition_values)

    grad_output_bias = bias_sums[:width]
    grad_down_bias = bias_sums[width : 2 * width]
    packed_sums = bias_sums[2 * width : 2 * width + 3 * cols]
    grad_attention_bias = jnp.stack([packed_sums[:cols], packed_sums[2 * cols :]])
    grad_up_bias = bias_sums[2 * width + 3 * cols :]
    return (
        outputs,
        grad_inputs,
        grad_conditions,
        grad_modulation_weight,
        grad_modulation_bias,
        grad_attention.reshape(depth, 3, cols),
        grad_attention_bias,
        grad_output,
        grad_output_bias,
        feed_grads[:, hidden:],
        grad_up_bias,
        feed_grads[:, :hidden].T,
        grad_down_bias,
    )


def solution(mesh):
    placed = (
        P(("fsdp", "tp"), None),
        P("fsdp", None),
        P("fsdp", None, "tp"),
        P(None, "tp"),
        P("fsdp", None, "tp"),
        P(None, "tp"),
        P("tp", "fsdp"),
        P(),
        P("fsdp", "tp"),
        P("tp"),
        P("tp", "fsdp"),
        P(),
        P(("fsdp", "tp"), None),
    )
    return jax.shard_map(
        per_device,
        mesh=mesh,
        in_specs=placed,
        out_specs=(
            P(("fsdp", "tp"), None),
            P(("fsdp", "tp"), None),
            P("fsdp", None),
            P("fsdp", None, "tp"),
            P(None, "tp"),
            P("fsdp", None, "tp"),
            P(None, "tp"),
            P("tp", "fsdp"),
            P(),
            P("fsdp", "tp"),
            P("tp"),
            P("tp", "fsdp"),
            P(),
        ),
        check_vma=False,
    )
```

```python
import functools
import math

import jax
import jax.numpy as jnp
from jax import lax
from jax.experimental import pallas as pl
from jax.experimental.pallas import tpu as pltpu
from jax.sharding import PartitionSpec as P

HD = 72


EPS = 1e-06
LOG2E = math.log2(math.e)
VMEM_LIMIT = 48 * 1024 * 1024
TILE = 768
BOTH_LAST = (((1,), (1,)), ((), ()))
BOTH_FIRST = (((0,), (0,)), ((), ()))


def mm(a, b, dims=(((1,), (0,)), ((), ()))):
    return lax.dot_general(a, b, dims, preferred_element_type=jnp.float32)


def normalize(values):
    centred = values - jnp.mean(values, axis=-1, keepdims=True)
    inverse = lax.rsqrt(jnp.mean(centred * centred, axis=-1, keepdims=True) + EPS)
    return (centred * inverse, inverse)


def normalize_back(incoming, normed, inverse):
    first_mean = jnp.mean(incoming, axis=-1, keepdims=True)
    second_mean = jnp.mean(incoming * normed, axis=-1, keepdims=True)
    return inverse * (incoming - first_mean - normed * second_mean)


def modulate(normed, shift, scale):
    return (normed * (1.0 + scale) + shift).astype(jnp.bfloat16)


def silu_slope(values):
    sigmoid = jax.nn.sigmoid(values)
    return sigmoid * (1.0 + values * (1.0 - sigmoid))


def gelu_pair(values):
    root = math.sqrt(2.0 / math.pi)
    square = values * values
    bend = jnp.tanh(root * values * (1.0 + 0.044715 * square))
    half = 0.5 * (1.0 + bend)
    slope = half + 0.5 * values * (1.0 - bend * bend) * root * (1.0 + 3.0 * 0.044715 * square)
    return values * half, slope


def attend_kernel(start, packed_ref, out_ref, log_ref):
    rows, cols = out_ref.shape
    factor = LOG2E / math.sqrt(HD)
    pieces = []
    for head in range(cols // HD):
        at = head * HD
        queries = packed_ref[start : start + rows, at : at + HD]
        key_rows = packed_ref[:, cols + at : cols + at + HD]
        value_rows = packed_ref[:, 2 * cols + at : 2 * cols + at + HD]
        scores = mm(key_rows, queries, BOTH_LAST)
        top = jnp.max(scores, axis=0, keepdims=True)
        shares = jnp.exp2((scores - top) * factor)
        total = jnp.sum(shares, axis=0, keepdims=True)
        piece = mm(value_rows, shares.astype(jnp.bfloat16), BOTH_FIRST)
        pieces.append(piece / total)
        log_ref[head : head + 1, :] = top * factor + jnp.log2(total)
    out_ref[...] = jnp.concatenate(pieces, axis=0).T.astype(jnp.bfloat16)


def attend(packed, start, rows):
    length, width = packed.shape
    cols = width // 3
    heads = cols // HD
    return pl.pallas_call(
        functools.partial(attend_kernel, start),
        out_shape=(
            jax.ShapeDtypeStruct((rows, cols), jnp.bfloat16),
            jax.ShapeDtypeStruct((heads, rows), jnp.float32),
        ),
        in_specs=[pl.BlockSpec(memory_space=pltpu.VMEM)],
        out_specs=(pl.BlockSpec(memory_space=pltpu.VMEM),) * 2,
        compiler_params=pltpu.CompilerParams(vmem_limit_bytes=VMEM_LIMIT),
        cost_estimate=pl.CostEstimate(
            flops=4 * rows * length * 256 * heads,
            bytes_accessed=packed.size * 2 + rows * cols * 2,
            transcendentals=rows * length * heads,
        ),
    )(packed)


def attend_back_kernel(start, last, *refs):
    packed_ref, upstream_ref, weight_ref, heads_ref, log_ref = refs[:5]
    up_ref = refs[-1]
    rows, cols = up_ref.shape
    if last:
        query_ins, key_in, value_in, out_ref, sum_ref = refs[5:-5], *refs[-5:-1]
    else:
        query_ref, key_ref, value_ref = refs[5:-1]
    up_ref[...] = mm(upstream_ref[...], weight_ref[...]).astype(jnp.bfloat16)
    scale = 1.0 / math.sqrt(HD)
    factor = LOG2E * scale
    products = (up_ref[...].astype(jnp.float32) * heads_ref[...].astype(jnp.float32)).T
    pieces = []
    for head in range(cols // HD):
        at = head * HD
        here = slice(at, at + HD)
        queries = packed_ref[start : start + rows, at : at + HD]
        key_rows = packed_ref[:, cols + at : cols + at + HD]
        value_rows = packed_ref[:, 2 * cols + at : 2 * cols + at + HD]
        incoming = up_ref[:, here]
        inner = jnp.sum(products[here], axis=0, keepdims=True)
        scores = mm(key_rows, queries, BOTH_LAST)
        shares = jnp.exp2(scores * factor - log_ref[head : head + 1, :])
        grads = mm(value_rows, incoming, BOTH_LAST)
        score_grads = (shares * (grads - inner)).astype(jnp.bfloat16)
        value_grad = jnp.dot(shares.astype(jnp.bfloat16), incoming, preferred_element_type=jnp.float32)
        key_grad = jnp.dot(score_grads, queries, preferred_element_type=jnp.float32) * scale
        if last:
            value_grad += value_in[:, here]
            key_grad += key_in[:, here]
            out_ref[:, 2 * cols + at : 2 * cols + at + HD] = value_grad.astype(jnp.bfloat16)
            out_ref[:, cols + at : cols + at + HD] = key_grad.astype(jnp.bfloat16)
        else:
            value_ref[:, here] = value_grad
            key_ref[:, here] = key_grad
        pieces.append(mm(key_rows, score_grads, BOTH_FIRST) * scale)
    query_grad = jnp.concatenate(pieces, axis=0).T.astype(jnp.bfloat16)
    if last:
        for step, query_in in enumerate(query_ins):
            out_ref[step * rows : (step + 1) * rows, :cols] = query_in[...]
        out_ref[start : start + rows, :cols] = query_grad
        sum_ref[...] = jnp.sum(out_ref[...].astype(jnp.float32), axis=0, keepdims=True)
    else:
        query_ref[...] = query_grad


def attend_back(packed, start, upstream, weight, heads_low, logs, query_grads, sums, last):
    length, width = packed.shape
    cols = width // 3
    heads = cols // HD
    rows = upstream.shape[0]
    operands = (packed, upstream, weight, heads_low, logs)
    if last:
        operands += tuple(query_grads) + tuple(sums)
        shapes = (
            jax.ShapeDtypeStruct((length, width), jnp.bfloat16),
            jax.ShapeDtypeStruct((1, width), jnp.float32),
        )
    else:
        shapes = (
            jax.ShapeDtypeStruct((rows, cols), jnp.bfloat16),
            jax.ShapeDtypeStruct((length, cols), jnp.float32),
            jax.ShapeDtypeStruct((length, cols), jnp.float32),
        )
    return pl.pallas_call(
        functools.partial(attend_back_kernel, start, last),
        out_shape=shapes,
        in_specs=[pl.BlockSpec(memory_space=pltpu.VMEM)] * len(operands),
        out_specs=jax.tree.map(lambda _: pl.BlockSpec(memory_space=pltpu.VMEM), shapes),
        scratch_shapes=[pltpu.VMEM((rows, cols), jnp.bfloat16)],
        compiler_params=pltpu.CompilerParams(vmem_limit_bytes=VMEM_LIMIT),
        cost_estimate=pl.CostEstimate(
            flops=10 * rows * length * 256 * heads,
            bytes_accessed=packed.size * 2 + rows * cols * 6 + length * cols * 8,
            transcendentals=rows * length * heads,
        ),
    )(*operands)


def feed_kernel(second_ref, feed_ref, up_ref, down_ref, bias_ref, act_ref, pre_ref, sum_ref):
    act, slope = gelu_pair(mm(second_ref[...], up_ref[...]) + bias_ref[...])
    act_ref[...] = act.astype(jnp.bfloat16)
    low = (mm(feed_ref[...], down_ref[...]) * slope).astype(jnp.bfloat16)
    pre_ref[...] = low
    sum_ref[...] = jnp.sum(low.astype(jnp.float32), axis=0, keepdims=True)


def feed_forward(second, feed_grad, weights, bias):
    rows, width = second.shape
    hidden = weights.shape[1] // 2
    tile = TILE
    tiles = hidden // tile
    if hidden % tile:
        act, slope = gelu_pair(mm(second, weights[:, :hidden]) + bias)
        low = (mm(feed_grad, weights[:, hidden:]) * slope).astype(jnp.bfloat16)
        sums = jnp.sum(low, axis=0, keepdims=True, dtype=jnp.float32)
        return act.astype(jnp.bfloat16), low, sums
    whole = pl.BlockSpec((rows, width), lambda j: (0, 0))
    piece = pl.BlockSpec((rows, tile), lambda j: (0, j))
    line = pl.BlockSpec((1, tile), lambda j: (0, j))
    return pl.pallas_call(
        feed_kernel,
        grid=(tiles,),
        out_shape=(
            jax.ShapeDtypeStruct((rows, hidden), jnp.bfloat16),
            jax.ShapeDtypeStruct((rows, hidden), jnp.bfloat16),
            jax.ShapeDtypeStruct((1, hidden), jnp.float32),
        ),
        in_specs=[
            whole,
            whole,
            pl.BlockSpec((width, tile), lambda j: (0, j)),
            pl.BlockSpec((width, tile), lambda j: (0, j + tiles)),
            line,
        ],
        out_specs=(piece, piece, line),
        compiler_params=pltpu.CompilerParams(vmem_limit_bytes=VMEM_LIMIT),
        cost_estimate=pl.CostEstimate(
            flops=4 * rows * width * hidden,
            bytes_accessed=2 * (2 * second.size + weights.size + 2 * rows * hidden),
            transcendentals=rows * hidden,
        ),
    )(second, feed_grad, weights, weights, bias)


def feed_weight_kernel(tiles, feed_ref, second_ref, act_ref, pre_ref, out_ref):
    step = pl.program_id(0)

    @pl.when(step < tiles)
    def _():
        out_ref[...] = mm(feed_ref[...], act_ref[...], BOTH_FIRST).astype(jnp.bfloat16)

    @pl.when(step >= tiles)
    def _():
        out_ref[...] = mm(second_ref[...], pre_ref[...], BOTH_FIRST).astype(jnp.bfloat16)


def feed_weight_grads(feed_grad, second, act, pre):
    rows, width = second.shape
    hidden = act.shape[1]
    tile = TILE
    tiles = hidden // tile
    if hidden % tile:
        grads = [mm(feed_grad, act, BOTH_FIRST), mm(second, pre, BOTH_FIRST)]
        return jnp.concatenate(grads, axis=1).astype(jnp.bfloat16)
    whole = pl.BlockSpec((rows, width), lambda j: (0, 0))
    return pl.pallas_call(
        functools.partial(feed_weight_kernel, tiles),
        grid=(2 * tiles,),
        out_shape=jax.ShapeDtypeStruct((width, 2 * hidden), jnp.bfloat16),
        in_specs=[
            whole,
            whole,
            pl.BlockSpec((rows, tile), lambda j: (0, jnp.minimum(j, tiles - 1))),
            pl.BlockSpec((rows, tile), lambda j: (0, jnp.maximum(j - tiles, 0))),
        ],
        out_specs=pl.BlockSpec((width, tile), lambda j: (0, j)),
        compiler_params=pltpu.CompilerParams(vmem_limit_bytes=VMEM_LIMIT),
        cost_estimate=pl.CostEstimate(
            flops=4 * rows * width * hidden,
            bytes_accessed=4 * (second.size + act.size + width * hidden),
            transcendentals=0,
        ),
    )(feed_grad, second, act, pre)


def weight_kernel(first_ref, packed_ref, upstream_ref, heads_ref, out_ref):
    width, wide = out_ref.shape
    cut = packed_ref.shape[1]
    step = width // 3

    def body(index, carry):
        rows = pl.ds(pl.multiple_of(index * step, step), step)
        out_ref[rows, :cut] = mm(first_ref[:, rows], packed_ref[...], BOTH_FIRST).astype(jnp.bfloat16)
        out_ref[rows, cut:] = mm(upstream_ref[:, rows], heads_ref[...], BOTH_FIRST).astype(jnp.bfloat16)
        return carry

    lax.fori_loop(0, width // step, body, 0)


def weight_grads(first, packed, upstream, heads):
    width = first.shape[1]
    wide = packed.shape[1] + heads.shape[1]
    return pl.pallas_call(
        weight_kernel,
        out_shape=jax.ShapeDtypeStruct((width, wide), jnp.bfloat16),
        in_specs=[pl.BlockSpec(memory_space=pltpu.VMEM)] * 4,
        out_specs=pl.BlockSpec(memory_space=pltpu.VMEM),
        compiler_params=pltpu.CompilerParams(vmem_limit_bytes=VMEM_LIMIT),
        cost_estimate=pl.CostEstimate(
            flops=2 * first.shape[0] * width * wide,
            bytes_accessed=2 * (first.size + packed.size + upstream.size + heads.size + width * wide),
            transcendentals=0,
        ),
    )(first, packed, upstream, heads)


def swap(values):
    return lax.ppermute(values, "tp", [(0, 1), (1, 0)])


def gather_rows(own, paired):
    if paired:
        return [own, swap(own)]
    return [lax.all_gather(own, "tp", axis=0, tiled=True)]


def scatter_rows(parts, paired):
    if paired:
        return parts[0] + swap(parts[1].astype(jnp.bfloat16)).astype(jnp.float32)
    whole = jnp.concatenate(parts, axis=0).astype(jnp.bfloat16)
    return lax.psum_scatter(whole, "tp", scatter_dimension=0, tiled=True).astype(jnp.float32)


def gather_columns(own):
    if lax.axis_size("tp") == 2:
        other = swap(own)
        left = lax.axis_index("tp") == 0
        return jnp.concatenate([jnp.where(left, own, other), jnp.where(left, other, own)], axis=-1)
    return lax.all_gather(own, "tp", axis=own.ndim - 1, tiled=True)


def take_columns(whole):
    count = lax.axis_size("tp")
    piece = whole.shape[1] // count
    if count == 2:
        return jnp.where(lax.axis_index("tp") == 0, whole[:, :piece], whole[:, piece:])
    return lax.dynamic_slice_in_dim(whole, lax.axis_index("tp") * piece, piece, 1)


def sum_pair(values):
    if lax.axis_size("tp") == 2:
        return values + swap(values)
    return lax.psum(values, "tp")


def gather_blocks(shard):
    whole = lax.all_gather(shard[None], "fsdp", axis=0, tiled=True)
    return whole.reshape(-1, shard.shape[1])


def exchange(blocks):
    return lax.all_to_all(blocks, "fsdp", 0, 0, tiled=True)


def share(values):
    return exchange(jnp.broadcast_to(values[None], (lax.axis_size("fsdp"),) + values.shape))


def hop(values, z_step, x_step, core_step):
    planes = lax.axis_size("fsdp") // 4
    moves = []
    for source in range(4 * planes):
        z, x, core = source // 4, source // 2 % 2, source % 2
        target = ((z + z_step) % planes * 2 + (x + x_step) % 2) * 2 + (core + core_step) % 2
        moves.append((source, target))
    return lax.ppermute(values, "fsdp", moves)


def place():
    index = lax.axis_index("fsdp")
    return index // 4, index // 2 % 2, index % 2


def per_device(
    inputs,
    conditions,
    modulation_weight,
    modulation_bias,
    attention_weight,
    attention_bias,
    output_weight,
    output_bias,
    up_weight,
    up_bias,
    down_weight,
    down_bias,
    cotangent,
):
    tp = lax.axis_size("tp")
    rank = lax.axis_index("tp")
    fsdp = lax.axis_size("fsdp")
    local_rows, width = inputs.shape
    latents = conditions.shape[0]
    length = local_rows * tp // latents
    depth = attention_weight.shape[0]
    cols = attention_weight.shape[2]
    hidden = up_weight.shape[1]
    paired = tp == 2 and latents == 1
    f32 = jnp.float32
    bf16 = jnp.bfloat16

    first_shard = jnp.concatenate([attention_weight.reshape(depth, 3 * cols), output_weight.T], axis=1)
    first_weights = gather_blocks(first_shard)
    attention_all = first_weights[:, : 3 * cols]
    output_all = first_weights[:, 3 * cols :]
    feed_shard = jnp.concatenate([up_weight, down_weight.T], axis=1)

    inputs_parts = gather_rows(inputs, paired)

    condition_values = conditions.astype(f32)
    silu_low = jax.nn.silu(condition_values).astype(bf16)
    silu_rows = exchange(silu_low.reshape(latents, fsdp, depth).transpose(1, 0, 2))
    silu_rows = silu_rows.reshape(fsdp * latents, depth)
    modulation_flat = modulation_weight.reshape(depth, 6 * cols)
    partial = mm(silu_rows, modulation_flat).reshape(fsdp, latents, 6 * cols)
    own_columns = jnp.sum(exchange(partial), axis=0).reshape(latents, 6, cols)
    own_columns, inputs_parts = lax.optimization_barrier((own_columns, inputs_parts))
    modulation = gather_columns(own_columns + modulation_bias.astype(f32))
    feed_shard, modulation = lax.optimization_barrier((feed_shard, modulation))
    feed_weights = gather_blocks(feed_shard)
    up_all = feed_weights[:, :hidden]
    down_all = feed_weights[:, hidden:]
    own_modulation = modulation[0]
    if latents > 1:
        own_modulation = lax.dynamic_index_in_dim(
            modulation, rank * local_rows // length, 0, keepdims=False
        )

    def own_rows(group):
        return own_modulation[group][None]

    def all_rows(group):
        if latents == 1:
            return modulation[0, group][None]
        return jnp.repeat(modulation[:, group], length, axis=0)

    def sum_latents(values):
        return jnp.sum(values.reshape(latents, length, width), axis=1)

    def place_latent(values):
        total = jnp.sum(values, axis=0)[None]
        if latents == 1:
            return total
        mine = jnp.arange(latents)[:, None] == rank * local_rows // length
        return jnp.where(mine, total, 0.0)

    cotangent_late, inputs_parts = lax.optimization_barrier((cotangent, inputs_parts))
    inputs_all = jnp.concatenate(inputs_parts, axis=0)
    cotangent_parts = gather_rows(cotangent_late, paired)
    input_values = inputs.astype(f32)
    first_normed, first_inverse = normalize(input_values)
    first_normed_all, _ = normalize(inputs_all.astype(f32))
    first_all = modulate(first_normed_all, all_rows(0), all_rows(1))
    bias_rows = attention_bias.astype(f32)
    packed_bias = jnp.concatenate([bias_rows[0], jnp.zeros((cols,), f32), bias_rows[1]])
    packed = (mm(first_all, attention_all) + packed_bias).astype(bf16)
    packed, cotangent_parts = lax.optimization_barrier((packed, cotangent_parts))

    block = local_rows
    blocks = length // block
    group_blocks = latents * blocks
    packed_latents = [packed[n * length : (n + 1) * length] for n in range(latents)]
    heads_parts = [None] * group_blocks
    logs = [None] * group_blocks
    products = [None] * group_blocks
    for at in reversed(range(group_blocks)):
        latent, start = at // blocks, at % blocks * block
        heads_parts[at], logs[at] = attend(packed_latents[latent], start, block)
        products[at] = mm(heads_parts[at], output_all, BOTH_LAST)
    attention = scatter_rows(products, paired) + output_bias.astype(f32)
    mid = input_values + own_rows(2) * attention
    second_normed, second_inverse = normalize(mid)
    second_parts = gather_rows(modulate(second_normed, own_rows(3), own_rows(4)), paired)

    gate_all = all_rows(5)
    if paired:
        feed_parts = [(gate_all * part.astype(f32)).astype(bf16) for part in cotangent_parts]
    else:
        feed_parts = [(gate_all * cotangent_parts[0].astype(f32)).astype(bf16)]
    feed_all = jnp.concatenate(feed_parts, axis=0)
    second_all = jnp.concatenate(second_parts, axis=0)
    act_all, pre_all, pre_sum = feed_forward(
        second_all, feed_all, feed_weights, up_bias.astype(f32)[None]
    )
    feed_grads = feed_weight_grads(feed_all, second_all, act_all, pre_all)

    def scatter_weights(values):
        return lax.psum_scatter(
            values.astype(bf16), "fsdp", scatter_dimension=0, tiled=True
        ).astype(f32)

    feed_grads, act_all, pre_all = lax.optimization_barrier((feed_grads, act_all, pre_all))
    feed_grads = scatter_weights(feed_grads)
    rows_kept = local_rows if paired else local_rows * tp
    act_parts = [act_all[:rows_kept], act_all[rows_kept:]][: len(second_parts)]
    pre_parts = [pre_all[:rows_kept], pre_all[rows_kept:]][: len(second_parts)]
    feed_sums = [mm(part, down_all, BOTH_LAST) for part in act_parts]
    second_sums = [mm(part, up_all, BOTH_LAST) for part in pre_parts]

    second_grad = scatter_rows(second_sums, paired)
    upstream = cotangent.astype(f32)
    mid_grad = upstream + normalize_back(
        second_grad * (1.0 + own_rows(4)), second_normed, second_inverse
    )
    attention_low = (own_rows(2) * mid_grad).astype(bf16)
    upstream_parts = gather_rows(attention_low, paired)
    if paired:
        feed_sums[1] = feed_sums[1].astype(bf16)
        feed_sums[1], upstream_parts[1] = lax.optimization_barrier((feed_sums[1], upstream_parts[1]))
    feed = scatter_rows(feed_sums, paired) + down_bias.astype(f32)
    heads_upstream = upstream_parts
    if not paired:
        heads_upstream = [
            upstream_parts[0][n * block : (n + 1) * block] for n in range(group_blocks)
        ]
    packed_parts = []
    packed_sums = []
    for latent in range(latents):
        query_grads = []
        sums = (jnp.zeros((length, cols), f32),) * 2
        for step in range(blocks):
            at = latent * blocks + step
            result = attend_back(
                packed_latents[latent],
                step * block,
                heads_upstream[at],
                output_all,
                heads_parts[at],
                logs[at],
                query_grads,
                sums,
                step == blocks - 1,
            )
            if step < blocks - 1:
                query_grads.append(result[0])
                sums = result[1:] if step == 0 else tuple(map(jnp.add, sums, result[1:]))
        packed_parts.append(result[0])
        packed_sums.append(result[1])
    packed_low = packed_parts[0] if latents == 1 else jnp.concatenate(packed_parts, axis=0)
    packed_sum = jnp.sum(jnp.concatenate(packed_sums, axis=0), axis=0)
    first_grads = weight_grads(
        first_all,
        packed_low,
        jnp.concatenate(upstream_parts, axis=0),
        jnp.concatenate(heads_parts, axis=0),
    )
    first_grads, feed, packed_low = lax.optimization_barrier((first_grads, feed, packed_low))
    first_grads, feed_grads = lax.optimization_barrier((first_grads, feed_grads))
    first_grads = scatter_weights(first_grads)
    grad_attention = first_grads[:, : 3 * cols]
    grad_output = first_grads[:, 3 * cols :].T
    first_grad_all = mm(packed_low, attention_all, BOTH_LAST)

    own_feed = feed_parts[0]
    if not paired:
        own_feed = (own_rows(5) * upstream).astype(bf16)
    token_sums = jnp.stack(
        [
            sum_latents(first_grad_all),
            sum_latents(first_grad_all * first_normed_all),
            place_latent(mid_grad * attention),
            place_latent(second_grad),
            place_latent(second_grad * second_normed),
            place_latent(upstream * feed),
        ],
        axis=1,
    )
    token_sums = jnp.concatenate(
        [
            token_sums.reshape(latents * 6, width),
            jnp.sum(attention_low, axis=0, dtype=f32, keepdims=True),
            jnp.sum(own_feed, axis=0, dtype=f32, keepdims=True),
        ]
    )
    token_sums = sum_pair(token_sums)
    first_grad_all, token_sums = lax.optimization_barrier((first_grad_all, token_sums))
    if paired:
        first_grad_parts = [first_grad_all[:local_rows], first_grad_all[local_rows:]]
    else:
        first_grad_parts = [first_grad_all]
    first_grad = scatter_rows(first_grad_parts, paired)
    modulation_low = take_columns(token_sums[: latents * 6]).astype(bf16)
    sums = jnp.concatenate(
        [
            modulation_low.astype(f32).reshape(latents * 6 * cols),
            token_sums[latents * 6 :].reshape(2 * width),
            packed_sum,
            pre_sum[0],
        ]
    )
    shared = share(sums[None]).reshape(fsdp, -1)
    shared, first_grad, feed, feed_grads = lax.optimization_barrier(
        (shared, first_grad, feed, feed_grads)
    )
    outputs = (mid + own_rows(5) * feed).astype(bf16)
    modulation_all = shared[:, : latents * 6 * cols].reshape(fsdp * latents, 6 * cols).astype(bf16)
    bias_sums = jnp.sum(shared[:, latents * 6 * cols :], axis=0)
    grad_modulation_weight = mm(silu_rows, modulation_all, BOTH_FIRST).reshape(depth, 6, cols)
    grad_modulation_bias = jnp.sum(modulation_all, axis=0, dtype=f32).reshape(6, cols)
    silu_part = sum_pair(mm(modulation_all, modulation_flat, BOTH_LAST))
    silu_total = exchange(silu_part.reshape(fsdp, latents, depth))
    silu_total = silu_total.transpose(1, 0, 2).reshape(latents, width)
    grad_inputs = mid_grad + normalize_back(
        first_grad * (1.0 + own_rows(1)), first_normed, first_inverse
    )
    grad_conditions = silu_total * silu_slope(condition_values)

    grad_output_bias = bias_sums[:width]
    grad_down_bias = bias_sums[width : 2 * width]
    packed_sums = bias_sums[2 * width : 2 * width + 3 * cols]
    grad_attention_bias = jnp.stack([packed_sums[:cols], packed_sums[2 * cols :]])
    grad_up_bias = bias_sums[2 * width + 3 * cols :]
    return (
        outputs,
        grad_inputs,
        grad_conditions,
        grad_modulation_weight,
        grad_modulation_bias,
        grad_attention.reshape(depth, 3, cols),
        grad_attention_bias,
        grad_output,
        grad_output_bias,
        feed_grads[:, hidden:],
        grad_up_bias,
        feed_grads[:, :hidden].T,
        grad_down_bias,
    )


def solution(mesh):
    placed = (
        P(("fsdp", "tp"), None),
        P("fsdp", None),
        P("fsdp", None, "tp"),
        P(None, "tp"),
        P("fsdp", None, "tp"),
        P(None, "tp"),
        P("tp", "fsdp"),
        P(),
        P("fsdp", "tp"),
        P("tp"),
        P("tp", "fsdp"),
        P(),
        P(("fsdp", "tp"), None),
    )
    return jax.shard_map(
        per_device,
        mesh=mesh,
        in_specs=placed,
        out_specs=(
            P(("fsdp", "tp"), None),
            P(("fsdp", "tp"), None),
            P("fsdp", None),
            P("fsdp", None, "tp"),
            P(None, "tp"),
            P("fsdp", None, "tp"),
            P(None, "tp"),
            P("tp", "fsdp"),
            P(),
            P("fsdp", "tp"),
            P("tp"),
            P("tp", "fsdp"),
            P(),
        ),
        check_vma=False,
    )
```
